768 devices in a mesh: team: 128 (over x, z_lo, y), rep: 6 (over z_hi, core).
Axes of the slice: x: 4, y: 8, z: 12 (z_hi: 3, z_lo: 4; z = z_hi * 4 + z_lo), core: 2. Of those that a mesh axis runs over, the one named last changes fastest.
Arguments:
- features: bfloat16 [147456, 128], P('team'), may hold values from -6 to 6
- degrees: int32 [147456], P('team'), may hold values from 1 to 16
- tiles: bfloat16 [6, 147456, 1152], P('rep', 'team'), may hold values from -0.15625 to 0.15625
- pattern: int32 [6, 128], P('rep', 'team'), may hold values 0 or 1
- weight: bfloat16 [128, 256], replicated, may hold values from -0.5 to 0.5
- cotangent: bfloat16 [147456, 256], P('team'), may hold values from -6 to 6
Outputs:
- hidden: bfloat16 [147456, 256], P(('team', 'rep'))
- grad_features: bfloat16 [147456, 128], P(('team', 'rep'))
- grad_weight: float32 [128, 256], replicated
The draws below stay inside these ranges and needn't reach their ends.
All inputs are finite; a program needn't handle non-finite values. No bound on the sum of `pattern` on one device may be relied on, other than what follows from the above.
Results may differ from the reference program's by a relative error of at most 0.006.
Values may be sent and summed in bfloat16 or wider, within the bound.
No kernel may reach another device: no remote copies, remote signals or barrier semaphores. Data moves between devices by JAX's collectives and lax.ppermute only.
A program may use at most 32 MiB of HBM per device.

```python
import math
import jax
import jax.numpy as jnp
from jax import lax

F = 128
HID = 256
R = 1152
STOPS = 6
NODES = 147456
N_TEAM = 128


def touch_ends(values, key, smallest, high):
    longest = values.shape.index(max(values.shape))
    spots = []
    for shift in (0, 1):
        where = [jax.random.randint(jax.random.fold_in(key, axis), (), 0, length) for axis, length in enumerate(values.shape)]
        where[longest] = (where[longest] + shift) % values.shape[longest]
        spots.append(tuple(where))
    return values.at[spots[0]].set(smallest).at[spots[1]].set(high)


def block_levels(own_key, shape, cuts, low, high):
    gain = 1.0
    for axis_at, shards_of in cuts:
        steps = jax.random.uniform(jax.random.fold_in(jax.random.fold_in(own_key, 6), axis_at), (shards_of,), jnp.float32, low / len(cuts), high / len(cuts))
        gain = gain * jnp.repeat(jnp.exp(steps), shape[axis_at] // shards_of).reshape((-1,) + (1,) * (len(shape) - 1 - axis_at))
    return gain


def noise(own_key, extent, spread, most, split=(), dtype=jnp.bfloat16):
    level = block_levels(own_key, extent, split, -0.22, 0.18) if split else 1.0
    entries = jax.random.normal(own_key, extent, jnp.float32) * spread * level
    return jnp.minimum(jnp.maximum(entries, -most), most).astype(dtype)


def setup_inputs(seed: int = 0) -> dict:
    keys = jax.random.split(jax.random.key(seed), 7)
    features = noise(keys[0], (NODES, F), 1.0, 6.0, ((0, 128),))
    degrees = touch_ends(jax.random.randint(keys[1], (NODES,), 1, 17), jax.random.fold_in(keys[1], 1), 1, 16).astype(jnp.int32)
    tiles = noise(keys[2], (STOPS, NODES, R), (R * STOPS // 4) ** -0.5, 0.15625, ((0, 6), (1, 128)))
    pattern = touch_ends((jax.random.randint(keys[3], (STOPS, N_TEAM), 0, 4) < 3).astype(jnp.int32), jax.random.fold_in(keys[3], 1), 0, 1)
    weight = noise(keys[4], (F, HID), F ** -0.5, 0.5)
    cotangent = noise(keys[5], (NODES, HID), 1.0, 6.0, ((0, 128),))
    return dict(features=features, degrees=degrees, tiles=tiles, pattern=pattern, weight=weight, cotangent=cotangent)


def silu_grad(value):
    sig = jax.nn.sigmoid(value)
    return sig * (1.0 + value * (1.0 - sig))

def reference(features, degrees, tiles, pattern, weight, cotangent):
    inv_root = 1.0 / jnp.sqrt(degrees.astype(jnp.float32))
    source = (features.astype(jnp.float32) * inv_root[:, None]).astype(jnp.bfloat16)
    blocks = source.reshape(N_TEAM, R, F)
    totals = jnp.zeros((N_TEAM, R, F), jnp.float32)
    for stop_num in range(STOPS):
        shifted = jnp.roll(blocks, stop_num, axis=0)
        tile_now = tiles[stop_num].reshape(N_TEAM, R, R)
        term_now = jnp.einsum('tuv,tvf->tuf', tile_now.astype(jnp.float32), shifted.astype(jnp.float32))
        totals = totals + term_now * pattern[stop_num].astype(jnp.float32)[:, None, None]
    aggregated = (totals.reshape(NODES, F) * inv_root[:, None]).astype(jnp.bfloat16)
    pre_act = jnp.dot(aggregated, weight, preferred_element_type=jnp.float32)
    hidden = jax.nn.silu(pre_act).astype(jnp.bfloat16)
    slope_term = (cotangent.astype(jnp.float32) * silu_grad(pre_act)).astype(jnp.bfloat16)
    grad_weight = lax.dot_general(aggregated, slope_term, (((0,), (0,)), ((), ())), preferred_element_type=jnp.float32) * (1.0 / math.sqrt(NODES))
    message = (lax.dot_general(slope_term, weight, (((1,), (1,)), ((), ())), preferred_element_type=jnp.float32) * inv_root[:, None]).astype(jnp.bfloat16)
    msg_blocks = message.reshape(N_TEAM, R, F)
    back_sum = jnp.zeros((N_TEAM, R, F), jnp.float32)
    for stop_num in range(STOPS):
        tile_now = tiles[stop_num].reshape(N_TEAM, R, R)
        term_now = jnp.einsum('tuv,tuf->tvf', tile_now.astype(jnp.float32), msg_blocks.astype(jnp.float32))
        term_now = term_now * pattern[stop_num].astype(jnp.float32)[:, None, None]
        back_sum = back_sum + jnp.roll(term_now, -stop_num, axis=0)
    grad_features = (back_sum.reshape(NODES, F) * inv_root[:, None]).astype(jnp.bfloat16)
    return (hidden, grad_features, grad_weight)
```

```python
import math

import jax
import jax.numpy as jnp
from jax import lax
from jax.sharding import PartitionSpec as P

BF = jnp.bfloat16
F32 = jnp.float32


def local(features, degrees, tiles, pattern, weight, cotangent):
    teams = lax.axis_size("team")
    reps = lax.axis_size("rep")
    zs = reps // 2
    rep = lax.axis_index("rep")
    z, core = rep // 2, rep % 2
    rows, feat = features.shape
    hid = weight.shape[1]
    own = rows // reps
    half = zs * own

    def across(value, move):
        route = [(i * reps + s, (move(i, s)[0] % teams) * reps + move(i, s)[1]) for i in range(teams) for s in range(reps)]
        return lax.ppermute(value, ("team", "rep"), route)

    def swap_core(value):
        return lax.ppermute(value, "rep", [(s, s ^ 1) for s in range(reps)])

    def pick(array, which):
        return lax.dynamic_index_in_dim(array, which, 1, keepdims=False)

    inv_root = 1.0 / jnp.sqrt(degrees.astype(F32))
    inv_half = pick(inv_root.reshape(zs, 2, own), core).reshape(half)
    inv_own = lax.dynamic_slice_in_dim(inv_root, rep * own, own, 0)
    source = (features.astype(F32) * inv_root[:, None]).astype(BF)
    tile_on = pattern[0, 0].astype(F32)
    tile = tiles[0]

    block = across(source, lambda i, s: (i + s, s))
    partial = jnp.dot(tile, block, preferred_element_type=F32) * tile_on
    parts = partial.reshape(zs, 2, own, feat)

    chip = pick(parts, core) + swap_core(pick(parts, 1 - core).astype(BF)).astype(F32)
    sent = chip.astype(BF)
    from1 = lax.ppermute(sent, "rep", [(s, (s + 2) % reps) for s in range(reps)])
    from2 = lax.ppermute(sent, "rep", [(s, (s + 4) % reps) for s in range(reps)])
    first = jnp.where(z == 0, sent, jnp.where(z == 1, from1, from2)).astype(F32)
    second = jnp.where(z == 1, sent, jnp.where(z == 2, from1, from2)).astype(F32)
    third = jnp.where(z == 2, sent, jnp.where(z == 0, from1, from2)).astype(F32)
    totals = (first + second + third).reshape(half, feat)

    aggregated = (totals * inv_half[:, None]).astype(BF)
    pre_act = jnp.dot(aggregated, weight, preferred_element_type=F32)
    sig = jax.nn.sigmoid(pre_act)
    hidden_half = (pre_act * sig).astype(BF)
    hidden = lax.dynamic_slice_in_dim(hidden_half, z * own, own, 0)
    cot_half = pick(cotangent.reshape(zs, 2, own, hid), core).reshape(half, hid)
    slope = (cot_half.astype(F32) * (sig * (1.0 + pre_act * (1.0 - sig)))).astype(BF)
    grad_part = lax.dot_general(aggregated, slope, (((0,), (0,)), ((), ())), preferred_element_type=F32)
    message_half = (
        lax.dot_general(slope, weight, (((1,), (1,)), ((), ())), preferred_element_type=F32) * inv_half[:, None]
    ).astype(BF)

    message_other = swap_core(message_half)
    mine, other = message_half.reshape(zs, 1, own, feat), message_other.reshape(zs, 1, own, feat)
    even, odd = jnp.where(core == 0, mine, other), jnp.where(core == 0, other, mine)
    message = jnp.concatenate([even, odd], axis=1).reshape(rows, feat)

    grad_parts = grad_part.reshape(2, feat // 2, hid)
    grad = lax.dynamic_index_in_dim(grad_parts, core, 0, keepdims=False) + swap_core(
        lax.dynamic_index_in_dim(grad_parts, 1 - core, 0, keepdims=False)
    )
    bit = 1
    while bit < teams:
        grad = grad + lax.ppermute(grad, "team", [(i, i ^ bit) for i in range(teams)])
        bit *= 2
    grad = grad * (1.0 / math.sqrt(rows * teams))
    grad_other = swap_core(grad)
    grad_weight = jnp.concatenate(
        [jnp.where(core == 0, grad, grad_other), jnp.where(core == 0, grad_other, grad)], axis=0
    )

    back = lax.dot_general(tile, message, (((0,), (0,)), ((), ())), preferred_element_type=F32) * tile_on
    backs = back.reshape(zs, 2, own, feat)
    pair = pick(backs, core) + across(
        pick(backs, 1 - core).astype(BF), lambda i, s: (i + 1 if s % 2 == 0 else i - 1, s ^ 1)
    ).astype(F32)
    sent = pair.astype(BF)
    summed = 0.0
    for k in range(zs):
        chunk = lax.dynamic_index_in_dim(sent, (z + k) % zs, 0, keepdims=False)
        summed = summed + across(chunk, lambda i, s: (i - s, 2 * ((s // 2 + k) % zs) + s % 2)).astype(F32)
    grad_features = (summed * inv_own[:, None]).astype(BF)
    return (hidden, grad_features, grad_weight)


def solution(mesh):
    in_specs = (
        P("team", None),
        P("team"),
        P("rep", "team", None),
        P("rep", "team"),
        P(),
        P("team", None),
    )
    out_specs = (P(("team", "rep"), None), P(("team", "rep"), None), P())
    return jax.shard_map(local, mesh=mesh, in_specs=in_specs, out_specs=out_specs, check_vma=False)
```

```python
import math

import jax
import jax.numpy as jnp
from jax import lax
from jax.sharding import PartitionSpec as P

BF = jnp.bfloat16
F32 = jnp.float32


def local(features, degrees, tiles, pattern, weight, cotangent):
    teams = lax.axis_size("team")
    reps = lax.axis_size("rep")
    zs = reps // 2
    rep = lax.axis_index("rep")
    z, core = rep // 2, rep % 2
    rows, feat = features.shape
    hid = weight.shape[1]
    own = rows // reps
    half = zs * own

    def across(value, move):
        route = [(i * reps + s, (move(i, s)[0] % teams) * reps + move(i, s)[1]) for i in range(teams) for s in range(reps)]
        return lax.ppermute(value, ("team", "rep"), route)

    def swap_core(value):
        return lax.ppermute(value, "rep", [(s, s ^ 1) for s in range(reps)])

    def pair_move(i, s):
        return (i + 1 if s % 2 == 0 else i - 1, s ^ 1)

    def pick(array, which):
        return lax.dynamic_index_in_dim(array, which, 1, keepdims=False)

    inv_root = 1.0 / jnp.sqrt(degrees.astype(F32))
    inv_half = pick(inv_root.reshape(zs, 2, own), core).reshape(half)
    inv_own = lax.dynamic_slice_in_dim(inv_root, rep * own, own, 0)
    source = (features.astype(F32) * inv_root[:, None]).astype(BF)
    tile_on = pattern[0, 0].astype(F32)
    tile = tiles[0]

    mid = rows // 2
    sent = lax.dynamic_slice_in_dim(source, core * mid, mid, 0)
    held = across(sent, lambda i, s: (i + s, s))
    other = across(held, pair_move)
    block = jnp.concatenate([jnp.where(core == 0, held, other), jnp.where(core == 0, other, held)], axis=0)
    partial = jnp.dot(tile, block, preferred_element_type=F32) * tile_on
    parts = partial.reshape(zs, 2, own, feat)

    chip = pick(parts, core) + swap_core(pick(parts, 1 - core).astype(BF)).astype(F32)
    sent = chip.astype(BF)
    from1 = lax.ppermute(sent, "rep", [(s, (s + 2) % reps) for s in range(reps)])
    from2 = lax.ppermute(sent, "rep", [(s, (s + 4) % reps) for s in range(reps)])
    first = jnp.where(z == 0, sent, jnp.where(z == 1, from1, from2)).astype(F32)
    second = jnp.where(z == 1, sent, jnp.where(z == 2, from1, from2)).astype(F32)
    third = jnp.where(z == 2, sent, jnp.where(z == 0, from1, from2)).astype(F32)
    totals = (first + second + third).reshape(half, feat)

    agg_half = (totals * inv_half[:, None]).astype(BF)
    agg_other = swap_core(agg_half)
    mine, other = agg_half.reshape(zs, 1, own, feat), agg_other.reshape(zs, 1, own, feat)
    even, odd = jnp.where(core == 0, mine, other), jnp.where(core == 0, other, mine)
    aggregated = jnp.concatenate([even, odd], axis=1).reshape(rows, feat)

    pre_act = jnp.dot(aggregated, weight, preferred_element_type=F32)
    sig = jax.nn.sigmoid(pre_act)
    hidden = lax.dynamic_slice_in_dim((pre_act * sig).astype(BF), rep * own, own, 0)
    slope = (cotangent.astype(F32) * (sig * (1.0 + pre_act * (1.0 - sig)))).astype(BF)
    message = (
        lax.dot_general(slope, weight, (((1,), (1,)), ((), ())), preferred_element_type=F32) * inv_root[:, None]
    ).astype(BF)
    grad_part = lax.dot_general(aggregated, slope, (((0,), (0,)), ((), ())), preferred_element_type=F32)

    grad = lax.dynamic_slice_in_dim(grad_part, core * (feat // 2), feat // 2, 0)

    def pair_sum(value, bit):
        return value + lax.ppermute(value, "team", [(i, i ^ bit) for i in range(teams)])

    bits = [1 << b for b in range((teams - 1).bit_length())]
    grad = pair_sum(grad, bits[0])
    back = lax.dot_general(tile, message, (((0,), (0,)), ((), ())), preferred_element_type=F32) * tile_on
    backs = back.reshape(zs, 2, own, feat)
    keep, give = pick(backs, core), pick(backs, 1 - core).astype(BF)
    grad, keep, give = lax.optimization_barrier((grad, keep, give))
    taken = across(give, pair_move)
    grad = pair_sum(grad, bits[1])
    sent = (keep + taken.astype(F32)).astype(BF)
    grad, sent = lax.optimization_barrier((grad, sent))
    got = []
    for k in range(zs):
        chunk = lax.dynamic_index_in_dim(sent, (z + k) % zs, 0, keepdims=False)
        got.append(across(chunk, lambda i, s: (i - s, 2 * ((s // 2 + k) % zs) + s % 2)))
    for bit in bits[2:4]:
        grad = pair_sum(grad, bit)
    grad, got = lax.optimization_barrier((grad, got))
    summed = sum(g.astype(F32) for g in got)
    grad_features = (summed * inv_own[:, None]).astype(BF)
    for bit in bits[4:]:
        grad = pair_sum(grad, bit)
    grad = grad * (1.0 / math.sqrt(rows * teams))
    grad_other = swap_core(grad)
    grad_weight = jnp.concatenate(
        [jnp.where(core == 0, grad, grad_other), jnp.where(core == 0, grad_other, grad)], axis=0
    )
    return (hidden, grad_features, grad_weight)


def solution(mesh):
    in_specs = (
        P("team", None),
        P("team"),
        P("rep", "team", None),
        P("rep", "team"),
        P(),
        P("team", None),
    )
    out_specs = (P(("team", "rep"), None), P(("team", "rep"), None), P())
    return jax.shard_map(local, mesh=mesh, in_specs=in_specs, out_specs=out_specs, check_vma=False)
```

```python
import math

import jax
import jax.numpy as jnp
from jax import lax
from jax.sharding import PartitionSpec as P

BF = jnp.bfloat16
F32 = jnp.float32


def local(features, degrees, tiles, pattern, weight, cotangent):
    teams = lax.axis_size("team")
    reps = lax.axis_size("rep")
    zs = reps // 2
    rep = lax.axis_index("rep")
    z, core = rep // 2, rep % 2
    rows, feat = features.shape
    hid = weight.shape[1]
    own = rows // reps
    half = zs * own

    def across(value, move):
        route = [(i * reps + s, (move(i, s)[0] % teams) * reps + move(i, s)[1]) for i in range(teams) for s in range(reps)]
        return lax.ppermute(value, ("team", "rep"), route)

    def swap_core(value):
        return lax.ppermute(value, "rep", [(s, s ^ 1) for s in range(reps)])

    def pick(array, which):
        return lax.dynamic_index_in_dim(array, which, 1, keepdims=False)

    inv_root = 1.0 / jnp.sqrt(degrees.astype(F32))
    inv_half = pick(inv_root.reshape(zs, 2, own), core).reshape(half)
    inv_own = lax.dynamic_slice_in_dim(inv_root, rep * own, own, 0)
    source = (features.astype(F32) * inv_root[:, None]).astype(BF)
    tile_on = pattern[0, 0].astype(F32)
    tile = tiles[0]

    block = across(source, lambda i, s: (i + s, s))
    partial = jnp.dot(tile, block, preferred_element_type=F32) * tile_on
    parts = partial.reshape(zs, 2, own, feat)

    chip = pick(parts, core) + swap_core(pick(parts, 1 - core).astype(BF)).astype(F32)
    sent = chip.astype(BF)
    from1 = lax.ppermute(sent, "rep", [(s, (s + 2) % reps) for s in range(reps)])
    from2 = lax.ppermute(sent, "rep", [(s, (s + 4) % reps) for s in range(reps)])
    first = jnp.where(z == 0, sent, jnp.where(z == 1, from1, from2)).astype(F32)
    second = jnp.where(z == 1, sent, jnp.where(z == 2, from1, from2)).astype(F32)
    third = jnp.where(z == 2, sent, jnp.where(z == 0, from1, from2)).astype(F32)
    totals = (first + second + third).reshape(half, feat)

    agg_half = (totals * inv_half[:, None]).astype(BF)
    agg_other = swap_core(agg_half)
    mine, other = agg_half.reshape(zs, 1, own, feat), agg_other.reshape(zs, 1, own, feat)
    even, odd = jnp.where(core == 0, mine, other), jnp.where(core == 0, other, mine)
    aggregated = jnp.concatenate([even, odd], axis=1).reshape(rows, feat)

    pre_act = jnp.dot(aggregated, weight, preferred_element_type=F32)
    sig = jax.nn.sigmoid(pre_act)
    hidden = lax.dynamic_slice_in_dim((pre_act * sig).astype(BF), rep * own, own, 0)
    slope = (cotangent.astype(F32) * (sig * (1.0 + pre_act * (1.0 - sig)))).astype(BF)
    message = (
        lax.dot_general(slope, weight, (((1,), (1,)), ((), ())), preferred_element_type=F32) * inv_root[:, None]
    ).astype(BF)
    grad_part = lax.dot_general(aggregated, slope, (((0,), (0,)), ((), ())), preferred_element_type=F32)

    back = lax.dot_general(tile, message, (((0,), (0,)), ((), ())), preferred_element_type=F32) * tile_on
    back = back.astype(BF)

    lanes = hid // 2
    size = -(-2 * feat // (16 * reps)) * 16
    tall = jnp.concatenate(
        [grad_part[:, :lanes], grad_part[:, lanes:], jnp.zeros((reps * size - 2 * feat, lanes), F32)], axis=0
    )
    piece = lax.dynamic_slice_in_dim(tall, rep * size, size, 0)
    piece, back = lax.optimization_barrier((piece, back))
    returned = across(back, lambda i, s: (i - s, s))
    inner = math.gcd(teams, 8)
    bit = 1
    while bit < inner:
        piece = piece + lax.ppermute(piece, "team", [(i, i ^ bit) for i in range(teams)])
        bit *= 2
    piece, returned = lax.optimization_barrier((piece, returned))
    groups = [[b * inner + y for b in range(teams // inner)] for y in range(inner)]
    spread = jnp.broadcast_to(piece[None], (len(groups[0]), size, lanes))
    piece = lax.all_to_all(spread, "team", 0, 0, axis_index_groups=groups).sum(axis=0)
    piece = piece * (1.0 / math.sqrt(rows * teams))

    high = lax.reduce_precision(piece, 8, 7)
    packed = jnp.concatenate([high.astype(BF), (piece - high).astype(BF)], axis=0)
    payload = jnp.concatenate(
        [returned.reshape(reps, own, feat), jnp.broadcast_to(packed[None], (reps, 2 * size, lanes))], axis=1
    )
    got = lax.all_to_all(payload, "rep", 0, 0)
    summed = got[:, :own].astype(F32).sum(axis=0)
    grad_features = (summed * inv_own[:, None]).astype(BF)
    tall = (got[:, own : own + size].astype(F32) + got[:, own + size :].astype(F32)).reshape(reps * size, lanes)
    grad_weight = jnp.concatenate([tall[:feat], tall[feat : 2 * feat]], axis=1)
    return (hidden, grad_features, grad_weight)


def solution(mesh):
    in_specs = (
        P("team", None),
        P("team"),
        P("rep", "team", None),
        P("rep", "team"),
        P(),
        P("team", None),
    )
    out_specs = (P(("team", "rep"), None), P(("team", "rep"), None), P())
    return jax.shard_map(local, mesh=mesh, in_specs=in_specs, out_specs=out_specs, check_vma=False)
```

```python
import functools
import math

import jax
import jax.numpy as jnp
from jax import lax
from jax.experimental import pallas as pl
from jax.experimental.pallas import tpu as pltpu
from jax.sharding import PartitionSpec as P

BF = jnp.bfloat16
F32 = jnp.float32


def forward_kernel(own, here_ref, tile_ref, block_ref, keep_ref, give_ref):
    core, tile_on = here_ref[0], here_ref[2].astype(F32)
    for q in range(keep_ref.shape[0]):
        for out_ref, side in ((keep_ref, core), (give_ref, 1 - core)):
            start = pl.multiple_of((2 * q + side) * own, own)
            term = jnp.dot(tile_ref[pl.ds(start, own), :], block_ref[...], preferred_element_type=F32)
            out_ref[q] = (term * tile_on).astype(out_ref.dtype)


def middle_kernel(
    own, size, here_ref, tile_ref, half_ref, other_ref, cot_ref, weight_ref, inv_ref,
    hidden_ref, keep_ref, give_ref, spread_ref, agg, slope, back, tall,
):
    core, rep, tile_on = here_ref[0], here_ref[1], here_ref[2].astype(F32)
    rows, feat = agg.shape
    lanes = tall.shape[1]
    zs = rows // (2 * own)
    weight = weight_ref[...]
    for q in range(zs):
        for in_ref, side in ((half_ref, core), (other_ref, 1 - core)):
            agg[pl.ds(pl.multiple_of((2 * q + side) * own, own), own), :] = in_ref[q * own : (q + 1) * own, :]
    grad = jnp.zeros((feat, weight.shape[1]), F32)
    for q in range(2 * zs):
        part = agg[q * own : (q + 1) * own, :]
        pre_act = jnp.dot(part, weight, preferred_element_type=F32)
        sig = jax.nn.sigmoid(pre_act)
        cot = cot_ref[q * own : (q + 1) * own, :].astype(F32)
        term = (cot * (sig * (1.0 + pre_act * (1.0 - sig)))).astype(BF)
        slope[q * own : (q + 1) * own, :] = term
        grad = grad + lax.dot_general(part, term, (((0,), (0,)), ((), ())), preferred_element_type=F32)
    message = lax.dot_general(weight, slope[...], (((1,), (1,)), ((), ())), preferred_element_type=F32)
    message = (message * inv_ref[...]).astype(BF)
    back[...] = (jnp.dot(message, tile_ref[...], preferred_element_type=F32) * tile_on).T
    for q in range(zs):
        for out_ref, side in ((keep_ref, core), (give_ref, 1 - core)):
            start = pl.multiple_of((2 * q + side) * own, own)
            out_ref[q] = back[pl.ds(start, own), :].astype(out_ref.dtype)
    tall[:feat, :] = grad[:, :lanes]
    tall[feat : 2 * feat, :] = grad[:, lanes:]
    tall[2 * feat :, :] = jnp.zeros((tall.shape[0] - 2 * feat, lanes), F32)
    piece = tall[pl.ds(pl.multiple_of(rep * size, size), size), :]
    for q in range(spread_ref.shape[0]):
        spread_ref[q] = piece
    pre_act = jnp.dot(agg[pl.ds(pl.multiple_of(rep * own, own), own), :], weight, preferred_element_type=F32)
    hidden_ref[...] = (pre_act * jax.nn.sigmoid(pre_act)).astype(BF)


def in_vmem(body, outs, scratch=()):
    def call(here, *arrays):
        vmem = pl.BlockSpec(memory_space=pltpu.VMEM)
        return pl.pallas_call(
            body,
            out_shape=[jax.ShapeDtypeStruct(shape, dtype) for shape, dtype in outs],
            in_specs=[pl.BlockSpec(memory_space=pltpu.SMEM)] + [vmem] * len(arrays),
            out_specs=[vmem] * len(outs),
            scratch_shapes=[pltpu.VMEM(shape, dtype) for shape, dtype in scratch],
            compiler_params=pltpu.CompilerParams(vmem_limit_bytes=10 * 2**20),
        )(here, *arrays)

    return call


def local(features, degrees, tiles, pattern, weight, cotangent):
    teams = lax.axis_size("team")
    reps = lax.axis_size("rep")
    zs = reps // 2
    rep = lax.axis_index("rep")
    z, core = rep // 2, rep % 2
    rows, feat = features.shape
    hid = weight.shape[1]
    own = rows // reps
    half = zs * own

    def across(value, move):
        route = [(i * reps + s, (move(i, s)[0] % teams) * reps + move(i, s)[1]) for i in range(teams) for s in range(reps)]
        return lax.ppermute(value, ("team", "rep"), route)

    def swap_core(value):
        return lax.ppermute(value, "rep", [(s, s ^ 1) for s in range(reps)])

    def pick(array, which):
        return lax.dynamic_index_in_dim(array, which, 1, keepdims=False)

    inv_root = 1.0 / jnp.sqrt(degrees.astype(F32))
    inv_half = pick(inv_root.reshape(zs, 2, own), core).reshape(half)
    inv_own = lax.dynamic_slice_in_dim(inv_root, rep * own, own, 0)
    source = (features.astype(F32) * inv_root[:, None]).astype(BF)
    tile = tiles[0]

    block = across(source, lambda i, s: (i + s, s))
    here = jnp.stack([core, rep, pattern[0, 0]]).astype(jnp.int32)
    halves = [((zs, own, feat), F32), ((zs, own, feat), BF)]
    keep, give = in_vmem(functools.partial(forward_kernel, own), halves)(here, tile, block)

    chip = keep + swap_core(give).astype(F32)
    sent = chip.astype(BF)
    trio = [[2 * k + c for k in range(zs)] for c in range(2)]
    chips = lax.all_gather(sent, "rep", axis_index_groups=trio).astype(F32)
    totals = chips.sum(axis=0).reshape(half, feat)

    agg_half = (totals * inv_half[:, None]).astype(BF)
    agg_other = swap_core(agg_half)

    lanes = hid // 2
    size = -(-2 * feat // (16 * reps)) * 16
    inner = math.gcd(teams, 8)
    hidden, keep, give, spread = in_vmem(
        functools.partial(middle_kernel, own, size),
        [((own, hid), BF), *halves, ((teams // inner, size, lanes), F32)],
        [((rows, feat), BF), ((rows, hid), BF), ((rows, feat), F32), ((reps * size, lanes), F32)],
    )(here, tile, agg_half, agg_other, cotangent, weight, inv_root[None, :])

    taken = across(give, lambda i, s: (i + 1 if s % 2 == 0 else i - 1, s ^ 1))
    apart = [[b * inner + y for b in range(teams // inner)] for y in range(inner)]
    near = [[b * inner + y for y in range(inner)] for b in range(teams // inner)]

    def sum_over(value, groups):
        return lax.all_to_all(value, "team", 0, 0, axis_index_groups=groups).sum(axis=0)

    def send(value, k):
        return across(value, lambda i, s: (i - s, 2 * ((s // 2 + k) % zs) + s % 2))

    piece = sum_over(spread, apart)
    sent = (keep + taken.astype(F32)).astype(BF)
    piece, sent = lax.optimization_barrier((piece, sent))
    chunks = [lax.dynamic_index_in_dim(sent, (z + k) % zs, 0, keepdims=False) for k in range(zs)]
    spread = jnp.broadcast_to(piece[None], (inner, size, lanes))
    piece = sum_over(spread, near) * (1.0 / math.sqrt(rows * teams))

    high = lax.reduce_precision(piece, 8, 7)
    packed = jnp.concatenate([high.astype(BF), (piece - high).astype(BF)], axis=0)
    stay = send(chunks[0], 0)
    got = [send(jnp.concatenate([chunks[k], packed], axis=0), k) for k in range(1, zs)]
    summed = stay.astype(F32) + sum(g[:own].astype(F32) for g in got)
    grad_features = (summed * inv_own[:, None]).astype(BF)
    pieces = [packed] + [g[own:] for g in got]
    pieces = [p[:size].astype(F32) + p[size:].astype(F32) for p in pieces]
    mine = jnp.stack(
        [jnp.where(z == q, pieces[0], jnp.where(z == (q + 1) % zs, pieces[1], pieces[2])) for q in range(zs)], axis=0
    )
    other = swap_core(mine)
    tall = jnp.stack([jnp.where(core == 0, mine, other), jnp.where(core == 0, other, mine)], axis=1)
    tall = tall.reshape(reps * size, lanes)
    grad_weight = jnp.concatenate([tall[:feat], tall[feat : 2 * feat]], axis=1)
    return (hidden, grad_features, grad_weight)


def solution(mesh):
    in_specs = (
        P("team", None),
        P("team"),
        P("rep", "team", None),
        P("rep", "team"),
        P(),
        P("team", None),
    )
    out_specs = (P(("team", "rep"), None), P(("team", "rep"), None), P())
    return jax.shard_map(local, mesh=mesh, in_specs=in_specs, out_specs=out_specs, check_vma=False)
```

```python
import functools
import math

import jax
import jax.numpy as jnp
from jax import lax
from jax.experimental import pallas as pl
from jax.experimental.pallas import tpu as pltpu
from jax.sharding import PartitionSpec as P

BF = jnp.bfloat16
F32 = jnp.float32


def split_kernel(own, here_ref, term_ref, keep_ref, give_ref, rows_ref):
    core, tile_on = here_ref[0], here_ref[2].astype(F32)
    rows_ref[...] = (term_ref[...] * tile_on).T
    for q in range(keep_ref.shape[0]):
        for out_ref, side in ((keep_ref, core), (give_ref, 1 - core)):
            start = pl.multiple_of((2 * q + side) * own, own)
            out_ref[q] = rows_ref[pl.ds(start, own), :].astype(out_ref.dtype)


def middle_kernel(
    own, size, here_ref, half_ref, other_ref, cot_ref, weight_ref, inv_ref,
    hidden_ref, message_ref, spread_ref, agg, slope, tall,
):
    core, rep = here_ref[0], here_ref[1]
    rows, feat = agg.shape
    lanes = tall.shape[1]
    zs = rows // (2 * own)
    weight = weight_ref[...]
    for q in range(zs):
        for in_ref, side in ((half_ref, core), (other_ref, 1 - core)):
            agg[pl.ds(pl.multiple_of((2 * q + side) * own, own), own), :] = in_ref[q * own : (q + 1) * own, :]
    grad = jnp.zeros((feat, weight.shape[1]), F32)
    for q in range(2 * zs):
        part = agg[q * own : (q + 1) * own, :]
        pre_act = jnp.dot(part, weight, preferred_element_type=F32)
        sig = jax.nn.sigmoid(pre_act)
        cot = cot_ref[q * own : (q + 1) * own, :].astype(F32)
        term = (cot * (sig * (1.0 + pre_act * (1.0 - sig)))).astype(BF)
        slope[q * own : (q + 1) * own, :] = term
        grad = grad + lax.dot_general(part, term, (((0,), (0,)), ((), ())), preferred_element_type=F32)
    message = lax.dot_general(weight, slope[...], (((1,), (1,)), ((), ())), preferred_element_type=F32)
    message_ref[...] = (message * inv_ref[...]).astype(BF)
    tall[:feat, :] = grad[:, :lanes]
    tall[feat : 2 * feat, :] = grad[:, lanes:]
    tall[2 * feat :, :] = jnp.zeros((tall.shape[0] - 2 * feat, lanes), F32)
    piece = tall[pl.ds(pl.multiple_of(rep * size, size), size), :]
    for q in range(spread_ref.shape[0]):
        spread_ref[q] = piece
    pre_act = jnp.dot(agg[pl.ds(pl.multiple_of(rep * own, own), own), :], weight, preferred_element_type=F32)
    hidden_ref[...] = (pre_act * jax.nn.sigmoid(pre_act)).astype(BF)


def in_vmem(body, outs, scratch=()):
    def call(here, *arrays):
        vmem = pl.BlockSpec(memory_space=pltpu.VMEM)
        return pl.pallas_call(
            body,
            out_shape=[jax.ShapeDtypeStruct(shape, dtype) for shape, dtype in outs],
            in_specs=[pl.BlockSpec(memory_space=pltpu.SMEM)] + [vmem] * len(arrays),
            out_specs=[vmem] * len(outs),
            scratch_shapes=[pltpu.VMEM(shape, dtype) for shape, dtype in scratch],
            compiler_params=pltpu.CompilerParams(vmem_limit_bytes=10 * 2**20),
        )(here, *arrays)

    return call


def local(features, degrees, tiles, pattern, weight, cotangent):
    teams = lax.axis_size("team")
    reps = lax.axis_size("rep")
    zs = reps // 2
    rep = lax.axis_index("rep")
    z, core = rep // 2, rep % 2
    rows, feat = features.shape
    hid = weight.shape[1]
    own = rows // reps
    half = zs * own

    def across(value, move):
        route = [(i * reps + s, (move(i, s)[0] % teams) * reps + move(i, s)[1]) for i in range(teams) for s in range(reps)]
        return lax.ppermute(value, ("team", "rep"), route)

    def swap_core(value):
        return lax.ppermute(value, "rep", [(s, s ^ 1) for s in range(reps)])

    inv_root = 1.0 / jnp.sqrt(degrees.astype(F32))

    def inv_rows(chunk):
        return jnp.broadcast_to(lax.dynamic_slice_in_dim(inv_root, chunk * own, own, 0)[:, None], (own, feat))

    inv_half, inv_own = jnp.concatenate([inv_rows(2 * q + core) for q in range(zs)], axis=0), inv_rows(rep)
    source = (features.astype(F32) * inv_root[:, None]).astype(BF)
    tile = tiles[0]

    block = across(source, lambda i, s: (i + s, s))
    block, inv_half, inv_own = lax.optimization_barrier((block, inv_half, inv_own))
    here = jnp.stack([core, rep, pattern[0, 0]]).astype(jnp.int32)
    halves = [((zs, own, feat), F32), ((zs, own, feat), BF)]
    split = in_vmem(functools.partial(split_kernel, own), halves, [((rows, feat), F32)])
    keep, give = split(here, lax.dot_general(block, tile, (((0,), (1,)), ((), ())), preferred_element_type=F32))

    chip = keep + swap_core(give).astype(F32)
    sent = chip.astype(BF)
    trio = [[2 * k + c for k in range(zs)] for c in range(2)]
    chips = lax.all_gather(sent, "rep", axis_index_groups=trio).astype(F32)
    totals = chips.sum(axis=0).reshape(half, feat)

    agg_half = (totals * inv_half).astype(BF)
    agg_other = swap_core(agg_half)

    lanes = hid // 2
    size = -(-2 * feat // (16 * reps)) * 16
    inner = math.gcd(teams, 8)
    hidden, message, spread = in_vmem(
        functools.partial(middle_kernel, own, size),
        [((own, hid), BF), ((feat, rows), BF), ((teams // inner, size, lanes), F32)],
        [((rows, feat), BF), ((rows, hid), BF), ((reps * size, lanes), F32)],
    )(here, agg_half, agg_other, cotangent, weight, inv_root[None, :])
    keep, give = split(here, jnp.dot(message, tile, preferred_element_type=F32))

    taken = across(give, lambda i, s: (i + 1 if s % 2 == 0 else i - 1, s ^ 1))
    apart = [[b * inner + y for b in range(teams // inner)] for y in range(inner)]
    near = [[b * inner + y for y in range(inner)] for b in range(teams // inner)]

    def sum_over(value, groups):
        return lax.all_to_all(value, "team", 0, 0, axis_index_groups=groups).sum(axis=0)

    def send(value, k):
        return across(value, lambda i, s: (i - s, 2 * ((s // 2 + k) % zs) + s % 2))

    piece = sum_over(spread, apart)
    sent = (keep + taken.astype(F32)).astype(BF)
    piece, sent = lax.optimization_barrier((piece, sent))
    chunks = [lax.dynamic_index_in_dim(sent, (z + k) % zs, 0, keepdims=False) for k in range(zs)]
    spread = jnp.broadcast_to(piece[None], (inner, size, lanes))
    piece = sum_over(spread, near) * (1.0 / math.sqrt(rows * teams))

    high = lax.reduce_precision(piece, 8, 7)
    packed = jnp.concatenate([high.astype(BF), (piece - high).astype(BF)], axis=0)
    stay = send(chunks[0], 0)
    got = [send(jnp.concatenate([chunks[k], packed], axis=0), k) for k in range(1, zs)]
    summed = stay.astype(F32) + sum(g[:own].astype(F32) for g in got)
    grad_features = (summed * inv_own).astype(BF)
    pieces = [packed] + [g[own:] for g in got]
    pieces = [p[:size].astype(F32) + p[size:].astype(F32) for p in pieces]
    mine = jnp.stack(
        [jnp.where(z == q, pieces[0], jnp.where(z == (q + 1) % zs, pieces[1], pieces[2])) for q in range(zs)], axis=0
    )
    other = swap_core(mine)
    tall = jnp.stack([jnp.where(core == 0, mine, other), jnp.where(core == 0, other, mine)], axis=1)
    tall = tall.reshape(reps * size, lanes)
    grad_weight = jnp.concatenate([tall[:feat], tall[feat : 2 * feat]], axis=1)
    return (hidden, grad_features, grad_weight)


def solution(mesh):
    in_specs = (
        P("team", None),
        P("team"),
        P("rep", "team", None),
        P("rep", "team"),
        P(),
        P("team", None),
    )
    out_specs = (P(("team", "rep"), None), P(("team", "rep"), None), P())
    return jax.shard_map(local, mesh=mesh, in_specs=in_specs, out_specs=out_specs, check_vma=False)
```
